32 devices in a mesh: row: 8 (over z, x), col: 2 (over y), zs: 2 (over core).
Axes of the slice: x: 2, y: 2, z: 4, core: 2. Of those that a mesh axis runs over, the one named last changes fastest.
Arguments:
- field: bfloat16 [128, 128, 12, 128], P('row', 'col', 'zs'), parts along dimension 2, may hold values from -12 to 12
- norm_gain: float32 [128], replicated, may hold values from 0.5 to 1.5
- first_x: bfloat16 [128, 128], replicated, may hold values from -0.5 to 0.5
- second_x: bfloat16 [128, 256], replicated, may hold values from -0.5 to 0.5
- first_y: bfloat16 [128, 128], replicated, may hold values from -0.5 to 0.5
- second_y: bfloat16 [128, 256], replicated, may hold values from -0.5 to 0.5
- value_weight: bfloat16 [128, 128], replicated, may hold values from -0.5 to 0.5
- out_weight: bfloat16 [128, 128], replicated, may hold values from -0.5 to 0.5
Outputs:
- mixed: bfloat16 [128, 128, 12, 128], P('row', 'col', 'zs'), parts along dimension 2
The draws below stay inside these ranges and needn't reach their ends.
There are 2 independent parts, one for each index of `zs`. The reference program is written for one: setup_inputs(seed, part) draws one part's arguments, and reference() takes and returns one part's arrays. A program takes and returns all parts, laid end to end along the dimension named above; an argument that names none is the same for every part. Nothing has to cross between parts.
All inputs are finite; a program needn't handle non-finite values.
Results may differ from the reference program's by a relative error of at most 0.006.
Values may be sent and summed in bfloat16 or wider, within the bound.
No kernel may reach another device: no remote copies, remote signals or barrier semaphores. Data moves between devices by JAX's collectives and lax.ppermute only.
A program may use at most 64 MiB of HBM per device.

```python
import jax
import jax.numpy as jnp
from jax import lax

C = 128
H = 8
ZL = 6
DH = 16
X = 128
Y = 128


def draw_field(key, part):
    key = jax.random.fold_in(key, 11)
    keys = jax.random.split(key, 5)
    noise = jax.random.normal(keys[0], (X, Y, ZL, C), jnp.float32)
    offset_x = 2.0 * jax.random.normal(keys[1], (X, C), jnp.float32)
    offset_y = 2.0 * jax.random.normal(keys[2], (Y, C), jnp.float32)
    sign_y = (2 * jax.random.randint(keys[3], (Y,), 0, 2) - 1).astype(jnp.float32)
    sign_x = (2 * jax.random.randint(keys[4], (X,), 0, 2) - 1).astype(jnp.float32)
    values = noise + offset_x[:, None, None, :] * sign_y[None, :, None, None]
    values = values + offset_y[None, :, None, :] * sign_x[:, None, None, None]
    return jnp.clip(values, -12.0, 12.0).astype(jnp.bfloat16)


def centred(key, dims, scale, limit, held_as=jnp.bfloat16):
    return jnp.clip(scale * jax.random.normal(key, dims, jnp.float32), -limit, limit).astype(held_as)


def setup_inputs(seed: int = 0, part: int = 0) -> dict:
    arg_keys = jax.random.split(jax.random.key(seed), 9)
    part_keys = jax.random.split(jax.random.fold_in(arg_keys[8], part), 9)
    return {
        "field": draw_field(jax.random.fold_in(jax.random.fold_in(arg_keys[8], part), 71), part),
        "norm_gain": jnp.clip(1.0 + 0.1 * jax.random.normal(arg_keys[1], (C,), jnp.float32), 0.5, 1.5),
        "first_x": centred(arg_keys[2], (C, C), C ** -0.5, 0.5),
        "second_x": centred(arg_keys[3], (C, 2 * C), C ** -0.5, 0.5),
        "first_y": centred(arg_keys[4], (C, C), C ** -0.5, 0.5),
        "second_y": centred(arg_keys[5], (C, 2 * C), C ** -0.5, 0.5),
        "value_weight": centred(arg_keys[6], (C, C), C ** -0.5, 0.5),
        "out_weight": centred(arg_keys[7], (C, C), C ** -0.5, 0.5),
    }


EPS = 1e-05
HIGH = lax.Precision.HIGHEST

def normalize(slab, gain):
    values = slab.astype(jnp.float32)
    center = lax.optimization_barrier(jnp.mean(values, axis=-1, keepdims=True))
    spread = lax.optimization_barrier(jnp.mean((values - center) ** 2, axis=-1, keepdims=True))
    return ((values - center) * lax.rsqrt(spread + EPS) * gain).astype(jnp.bfloat16)

def project(normed, w_first, w_second):
    hidden = jax.nn.gelu(jnp.dot(normed, w_first, preferred_element_type=jnp.float32)).astype(jnp.bfloat16)
    return jnp.dot(hidden, w_second, preferred_element_type=jnp.float32)

def reference(field, norm_gain, first_x, second_x, first_y, second_y, value_weight, out_weight):

    def pooled(slab):
        normed = normalize(slab, norm_gain)
        along_x = project(normed, first_x, second_x)
        along_y = project(normed, first_y, second_y)
        return (lax.optimization_barrier(jnp.sum(along_x, axis=(0, 1))), lax.optimization_barrier(jnp.sum(along_y, axis=1)))
    sums_x, sums_y = lax.map(pooled, field)
    summary_x = sums_x / (Y * ZL)
    summary_y = lax.optimization_barrier(jnp.sum(sums_y, axis=0)) / (X * ZL)
    query_x = summary_x[:, :C].reshape(X, H, DH)
    key_x = summary_x[:, C:].reshape(X, H, DH)
    query_y = summary_y[:, :C].reshape(Y, H, DH)
    key_y = summary_y[:, C:].reshape(Y, H, DH)

    def accumulate(total, inputs):
        slab, key_row = inputs
        normed = normalize(slab, norm_gain)
        value = jnp.dot(normed, value_weight, preferred_element_type=jnp.float32).astype(jnp.bfloat16)
        value = value.reshape(Y, ZL, H, DH).astype(jnp.float32)
        return (total + jnp.einsum('hd,yzhe->yzhde', key_row, value, precision=HIGH), None)
    start = jnp.zeros((Y, ZL, H, DH, DH), jnp.float32)
    s_x, _ = lax.scan(accumulate, start, (field, key_x))

    def finish(query_row):
        u_x = jnp.einsum('hd,yzhde->yzhe', query_row, s_x, precision=HIGH) / jnp.sqrt(jnp.float32(X))
        s_y = jnp.einsum('yhd,yzhe->zhde', key_y, u_x, precision=HIGH)
        u_y = (jnp.einsum('yhd,zhde->yzhe', query_y, s_y, precision=HIGH) / jnp.sqrt(jnp.float32(Y))).astype(jnp.bfloat16)
        return jnp.dot(u_y.reshape(Y, ZL, C), out_weight, preferred_element_type=jnp.float32).astype(jnp.bfloat16)
    return lax.map(finish, query_x)
```

```python
import functools

import jax
import jax.numpy as jnp
from jax import lax
from jax.experimental import pallas as pl
from jax.experimental.pallas import tpu as pltpu
from jax.sharding import PartitionSpec as P

H = 8
EPS = 1e-05
HIGH = lax.Precision.HIGHEST
F32 = jnp.float32
BF16 = jnp.bfloat16
GELU_A = 0.7978845608028654
GELU_B = GELU_A * 0.044715
VMEM_LIMIT = 48 * 1024 * 1024


def dot(a, b):
    return jnp.dot(a, b, preferred_element_type=F32)


def halves(a):
    high = a.astype(BF16)
    return high, (a - high.astype(F32)).astype(BF16)


def spread(rows, depth):
    width = rows.shape[1]
    shape = (width, depth * width)
    source = lax.broadcasted_iota(jnp.int32, shape, 0)
    target = lax.broadcasted_iota(jnp.int32, shape, 1)
    lane = target % width
    pick = (source // depth == lane // depth) & (source % depth == target // width)
    return jnp.dot(rows, pick.astype(F32), precision=HIGH, preferred_element_type=F32)


def pooled_kernel(field_ref, gain_ref, first_ref, weight_ref, sum_x_ref, sum_y_ref, value_ref):
    x_local, z_local, y_local, width = field_ref.shape
    ones = jnp.full((width, width), 1.0 / width, BF16)
    ones_two = jnp.full((2 * width, width), 1.0 / width, BF16)
    gain = gain_ref[...]
    sum_y_ref[...] = jnp.zeros_like(sum_y_ref)

    def step(i, carry):
        slab = field_ref[i].reshape(z_local * y_local, width)
        centred = slab.astype(F32) - dot(slab, ones)
        high, low = halves(centred * centred)
        spread_ = dot(jnp.concatenate([high, low], axis=1), ones_two)
        normed = (centred * lax.rsqrt(spread_ + EPS) * gain).astype(BF16)
        h = dot(normed, first_ref[...])
        g = h + h * jnp.tanh(h * (GELU_A + GELU_B * (h * h)))
        sum_x_ref[pl.ds(i, 1), :] = jnp.sum(g[:, :width], axis=0, keepdims=True)
        sum_y_ref[...] += jnp.sum(g[:, width:].reshape(z_local, y_local, width), axis=0)
        value = dot(normed, weight_ref[...]).astype(BF16)
        for z in range(z_local):
            value_ref[i, :, z * width : (z + 1) * width] = value[z * y_local : (z + 1) * y_local]
        return carry

    lax.fori_loop(0, x_local, step, 0)


def outer_kernel(scale_x, scale_y, sum_x_ref, sum_y_ref, key_x_ref, key_y_ref, value_ref, total_ref, part_ref):
    x_local, y_local, lanes = value_ref.shape
    width = key_x_ref.shape[0]
    depth = width // H
    key_x = jnp.dot(sum_x_ref[...] * scale_x, key_x_ref[...].astype(F32), precision=HIGH)
    key_y = jnp.dot(sum_y_ref[...] * scale_y, key_y_ref[...].astype(F32), precision=HIGH)
    high, low = halves(key_y.T)
    left = jnp.concatenate([high, low], axis=0)
    spread_x = spread(key_x, depth)
    head = (lax.broadcasted_iota(jnp.int32, (depth, lanes), 1) % width) // depth

    for i in range(x_local):
        both = dot(left, value_ref[i])
        both = both[:width] + both[width:]
        acc = both[:depth]
        for h in range(1, H):
            acc = jnp.where(head == h, both[h * depth : (h + 1) * depth], acc)
        part_ref[i] = acc

    for d in range(depth):
        for z in range(lanes // width):
            cols = slice(z * width, (z + 1) * width)
            acc = jnp.zeros((depth, width), F32)
            for i in range(x_local):
                acc += spread_x[i : i + 1, d * width : (d + 1) * width] * part_ref[i, :, cols]
            total_ref[d * depth : (d + 1) * depth, cols] = acc.astype(BF16)


def finish_kernel(scale_x, scale_y, sum_x_ref, sum_y_ref, query_x_ref, query_y_ref, total_ref, weight_ref, out_ref):
    x_local, z_local, y_local, width = out_ref.shape
    depth = width // H
    lanes = z_local * width
    query_x = jnp.dot(sum_x_ref[...] * scale_x, query_x_ref[...].astype(F32), precision=HIGH)
    query_y = jnp.dot(sum_y_ref[...] * scale_y, query_y_ref[...].astype(F32), precision=HIGH)
    high, low = halves(query_y)
    left = jnp.concatenate([high, low, high], axis=1)
    spread_x = spread(query_x, depth)
    head = (lax.broadcasted_iota(jnp.int32, (depth, lanes), 1) % width) // depth
    zero = jnp.zeros((depth, lanes), BF16)

    for i in range(x_local):
        pieces = []
        for z in range(z_local):
            cols = slice(z * width, (z + 1) * width)
            acc = jnp.zeros((depth, width), F32)
            for d in range(depth):
                acc += spread_x[i : i + 1, d * width : (d + 1) * width] * total_ref[
                    d * depth : (d + 1) * depth, cols
                ].astype(F32)
            pieces.append(acc)
        w_high, w_low = halves(jnp.concatenate(pieces, axis=1))
        diag_high = jnp.concatenate([jnp.where(head == h, w_high, zero) for h in range(H)], axis=0)
        diag_low = jnp.concatenate([jnp.where(head == h, w_low, zero) for h in range(H)], axis=0)
        u = dot(left, jnp.concatenate([diag_high, diag_high, diag_low], axis=0)).astype(BF16)
        for z in range(z_local):
            out_ref[i, z] = dot(u[:, z * width : (z + 1) * width], weight_ref[...]).astype(BF16)


def call(kernel, out_shape, flops, scratch=()):
    return pl.pallas_call(
        kernel,
        out_shape=out_shape,
        scratch_shapes=list(scratch),
        compiler_params=pltpu.CompilerParams(vmem_limit_bytes=VMEM_LIMIT),
        cost_estimate=pl.CostEstimate(flops=flops, bytes_accessed=4 << 20, transcendentals=0),
    )


def pair_sum(value, axis):
    size = lax.axis_size(axis)
    bit = 1
    while bit < size:
        value = value + lax.ppermute(value, axis, [(i, i ^ bit) for i in range(size)])
        bit *= 2
    return value


def total_sum(part):
    axes = ("row", "col")
    n = lax.axis_size("row") * lax.axis_size("col")
    rows, lanes = part.shape
    blocks = lax.all_to_all(part.reshape(n, rows // n, lanes), axes, 0, 0)
    mine = jnp.sum(blocks.astype(F32), axis=0).astype(BF16)
    spread_ = jnp.broadcast_to(mine, blocks.shape)
    return lax.all_to_all(spread_, axes, 0, 0).reshape(rows, lanes)


def body(field, norm_gain, first_x, second_x, first_y, second_y, value_weight, out_weight):
    x_local, y_local, z_local, width = field.shape
    depth = width // H
    lanes = z_local * width
    total_x = x_local * lax.axis_size("row")
    total_y = y_local * lax.axis_size("col")
    sum_x, sum_y, value = call(
        pooled_kernel,
        [
            jax.ShapeDtypeStruct((x_local, width), F32),
            jax.ShapeDtypeStruct((y_local, width), F32),
            jax.ShapeDtypeStruct((x_local, y_local, lanes), BF16),
        ],
        1 << 30,
    )(
        jnp.transpose(field, (0, 2, 1, 3)),
        norm_gain.reshape(1, width),
        jnp.concatenate([first_x, first_y], axis=1),
        value_weight,
    )
    sum_x = pair_sum(sum_x, "col")
    sum_y = pair_sum(sum_y, "row")
    mean_x = 0.5 / (total_y * z_local)
    mean_y = 0.5 / (total_x * z_local)
    part = call(
        functools.partial(outer_kernel, mean_x, mean_y),
        jax.ShapeDtypeStruct((depth * depth, lanes), BF16),
        1 << 30,
        [pltpu.VMEM((x_local, depth, lanes), F32)],
    )(sum_x, sum_y, second_x[:, width:], second_y[:, width:], value)
    total = total_sum(part)
    out = call(
        functools.partial(finish_kernel, mean_x * total_x**-0.5, mean_y * total_y**-0.5),
        jax.ShapeDtypeStruct((x_local, z_local, y_local, width), BF16),
        1 << 30,
    )(sum_x, sum_y, second_x[:, :width], second_y[:, :width], total, out_weight)
    return jnp.transpose(out, (0, 2, 1, 3))


def solution(mesh):
    placed = (P("row", "col", "zs", None), P(), P(), P(), P(), P(), P(), P())
    return jax.shard_map(
        body, mesh=mesh, in_specs=placed, out_specs=P("row", "col", "zs", None), check_vma=False
    )
```

```python
import functools

import jax
import jax.numpy as jnp
from jax import lax
from jax.experimental import pallas as pl
from jax.experimental.pallas import tpu as pltpu
from jax.sharding import PartitionSpec as P

H = 8
EPS = 1e-05
HIGH = lax.Precision.HIGHEST
F32 = jnp.float32
BF16 = jnp.bfloat16
GELU_A = 0.7978845608028654
GELU_B = GELU_A * 0.044715
VMEM_LIMIT = 48 * 1024 * 1024
CHUNKS = 4
CUTS = (0, 4, 8, 12, 16)
GROUP = 8
LIMIT_A = 62 * 1024 * 1024
IN_HBM = pl.BlockSpec(memory_space=pltpu.HBM)


def dot(a, b):
    return jnp.dot(a, b, preferred_element_type=F32)


def halves(a):
    high = a.astype(BF16)
    return high, (a - high.astype(F32)).astype(BF16)


def summary(sums, scale, second):
    return jnp.dot(sums * scale, second.astype(F32), precision=HIGH)


def spread_into(ref, rows):
    width = rows.shape[1]
    depth = width // H
    start = lax.broadcasted_iota(jnp.int32, rows.shape, 1) // depth * depth
    for d in range(depth):
        ref[:, d * width : (d + 1) * width] = jnp.take_along_axis(rows, start + d, axis=1)


def gelu_twice(h):
    return h + h * jnp.tanh(h * (GELU_A + GELU_B * (h * h)))


def norm_kernel(field_hbm, gain_hbm, first_hbm, sum_y_ref, normed_hbm, field_ref, normed_ref, gain_ref, first_ref, sems):
    x_local, z_local, y_local, width = normed_ref.shape
    cuts = [x_local * k // 16 for k in CUTS]
    parts = [(a, b - a) for a, b in zip(cuts[:-1], cuts[1:])]
    count = len(parts)
    small = [
        pltpu.make_async_copy(gain_hbm, gain_ref, sems.at[2 * count]),
        pltpu.make_async_copy(first_hbm, first_ref, sems.at[2 * count + 1]),
    ]
    big = [
        pltpu.make_async_copy(field_hbm.at[pl.ds(a, n)], field_ref.at[pl.ds(a, n)], sems.at[c])
        for c, (a, n) in enumerate(parts)
    ]
    for copy in small + big:
        copy.start()
    for copy in small:
        copy.wait()
    gain = gain_ref[...]
    sum_y_ref[...] = jnp.zeros_like(sum_y_ref)
    outs = []

    for c, (a, n) in enumerate(parts):
        big[c].wait()
        part = pl.ds(a, n)
        values = field_ref[part].reshape(n * z_local * y_local, width).astype(F32)
        centred = values - jnp.mean(values, axis=-1, keepdims=True)
        spread = jnp.mean(centred * centred, axis=-1, keepdims=True)
        normed = (centred * lax.rsqrt(spread + EPS) * gain).astype(BF16)
        normed_ref[part] = normed.reshape(n, z_local, y_local, width)
        out = pltpu.make_async_copy(normed_ref.at[part], normed_hbm.at[part], sems.at[count + c])
        out.start()
        outs.append(out)
        g = gelu_twice(dot(normed, first_ref[...]))
        sum_y_ref[...] += jnp.sum(g.reshape(n * z_local, y_local, width), axis=0)
    for out in outs:
        out.wait()


def chunks_of(hbm, ref, sems):
    n = ref.shape[0] // CHUNKS
    copies = [
        pltpu.make_async_copy(hbm.at[pl.ds(c * n, n)], ref.at[pl.ds(c * n, n)], sems.at[c]) for c in range(CHUNKS)
    ]
    for copy in copies:
        copy.start()
    for c in range(CHUNKS):
        copies[c].wait()
        yield c * n, ref[pl.ds(c * n, n)].reshape(-1, ref.shape[3]), n


def sum_x_kernel(normed_hbm, first_hbm, sum_x_ref, normed_ref, first_ref, sems):
    load = pltpu.make_async_copy(first_hbm, first_ref, sems.at[CHUNKS])
    load.start()
    for start, rows, n in chunks_of(normed_hbm, normed_ref, sems):
        if start == 0:
            load.wait()
        g = gelu_twice(dot(rows, first_ref[...]))
        sum_x_ref[start : start + n, :] = jnp.sum(g.reshape(n, -1, g.shape[1]), axis=1)


def value_kernel(normed_hbm, weight_hbm, value_ref, normed_ref, weight_ref, sems):
    z_local, y_local, width = normed_ref.shape[1:]
    load = pltpu.make_async_copy(weight_hbm, weight_ref, sems.at[CHUNKS])
    load.start()
    for start, rows, n in chunks_of(normed_hbm, normed_ref, sems):
        if start == 0:
            load.wait()
        value = dot(rows, weight_ref[...]).astype(BF16).reshape(n, z_local, y_local, width)
        for z in range(z_local):
            value_ref[start : start + n, :, z * width : (z + 1) * width] = value[:, z]


def outer_kernel(scale_x, scale_y, sum_x_ref, sum_y_ref, key_x_ref, key_y_ref, value_ref, total_ref, part_ref, rows_ref):
    x_local, y_local, lanes = value_ref.shape
    width = key_x_ref.shape[0]
    depth = width // H
    key_y = summary(sum_y_ref[...], scale_y, key_y_ref[...])
    left = jnp.concatenate(halves(key_y.T), axis=1)
    spread_into(rows_ref, summary(sum_x_ref[...], scale_x, key_x_ref[...]))
    head = (lax.broadcasted_iota(jnp.int32, (depth, lanes), 1) % width) // depth

    def step(j, carry):
        group = [j * GROUP + q for q in range(GROUP)]
        fulls = [dot(left, jnp.concatenate([value_ref[i]] * 2, axis=0)) for i in group]
        for i, full in zip(group, fulls):
            acc = full[:depth]
            for h in range(1, H):
                acc = jnp.where(head == h, full[h * depth : (h + 1) * depth], acc)
            part_ref[i] = acc
        return carry

    lax.fori_loop(0, x_local // GROUP, step, 0)

    for z in range(lanes // width):
        cols = slice(z * width, (z + 1) * width)
        for d in range(depth):
            acc = jnp.zeros((depth, width), F32)
            for i in range(x_local):
                acc += rows_ref[i : i + 1, d * width : (d + 1) * width] * part_ref[i, :, cols]
            total_ref[d * depth : (d + 1) * depth, cols] = acc.astype(BF16)


def finish_kernel(
    scale_x, scale_y, sum_x_ref, sum_y_ref, query_x_ref, query_y_ref, total_ref, weight_ref,
    out_hbm, out_ref, wide_ref, rows_ref, sems,
):
    x_local, z_local, y_local, width = out_ref.shape
    depth = width // H
    lanes = z_local * width
    wide_ref[...] = total_ref[...].astype(F32)
    query_y = summary(sum_y_ref[...], scale_y, query_y_ref[...])
    high, low = halves(query_y)
    left = jnp.concatenate(
        [jnp.concatenate([high, high], axis=1), jnp.concatenate([low, jnp.zeros_like(low)], axis=1)], axis=0
    )
    spread_into(rows_ref, summary(sum_x_ref[...], scale_x, query_x_ref[...]))
    head = (lax.broadcasted_iota(jnp.int32, (depth, lanes), 1) % width) // depth
    zero = jnp.zeros((depth, lanes), BF16)

    def copy_of(i):
        return pltpu.make_async_copy(out_ref.at[i], out_hbm.at[i], sems.at[i])

    def right_of(i):
        pieces = []
        rows = rows_ref[pl.ds(i, 1), :]
        for z in range(z_local):
            cols = slice(z * width, (z + 1) * width)
            acc = jnp.zeros((depth, width), F32)
            for d in range(depth):
                acc += rows[:, d * width : (d + 1) * width] * wide_ref[d * depth : (d + 1) * depth, cols]
            pieces.append(acc)
        return jnp.concatenate(
            [jnp.where(head == h, w, zero) for w in halves(jnp.concatenate(pieces, axis=1)) for h in range(H)],
            axis=0,
        )

    def step(j, carry):
        group = [j * GROUP + q for q in range(GROUP)]
        boths = [dot(left, right) for right in [right_of(i) for i in group]]
        for i, both in zip(group, boths):
            u = (both[:y_local] + both[y_local:]).astype(BF16)
            u = jnp.concatenate([u[:, z * width : (z + 1) * width] for z in range(z_local)], axis=0)
            out_ref[i] = dot(u, weight_ref[...]).astype(BF16).reshape(z_local, y_local, width)
            copy_of(i).start()
        return carry

    lax.fori_loop(0, x_local // GROUP, step, 0)

    def finish(i, carry):
        copy_of(i).wait()
        return carry

    lax.fori_loop(0, x_local, finish, 0)


def call(kernel, out_shape, flops, scratch=(), limit=VMEM_LIMIT, **specs):
    return pl.pallas_call(
        kernel,
        out_shape=out_shape,
        scratch_shapes=list(scratch),
        compiler_params=pltpu.CompilerParams(vmem_limit_bytes=limit),
        cost_estimate=pl.CostEstimate(flops=flops, bytes_accessed=4 << 20, transcendentals=0),
        **specs,
    )


def exchange(value, axis, bit):
    return value + lax.ppermute(value, axis, [(i, i ^ bit) for i in range(lax.axis_size(axis))])


def pair_sums(sum_x, sum_y):
    sum_y = exchange(sum_y, "row", 1)
    sum_x, sum_y = lax.optimization_barrier((sum_x, sum_y))
    bit = 2
    while bit < lax.axis_size("row"):
        sum_y = exchange(sum_y, "row", bit)
        bit *= 2
    bit = 1
    while bit < lax.axis_size("col"):
        sum_x = exchange(sum_x, "col", bit)
        bit *= 2
    return sum_x, sum_y


def total_sum(part):
    axes = ("row", "col")
    n = lax.axis_size("row") * lax.axis_size("col")
    rows, lanes = part.shape
    blocks = lax.all_to_all(part.reshape(n, rows // n, lanes), axes, 0, 0)
    mine = jnp.sum(blocks.astype(F32), axis=0).astype(BF16)
    spread = jnp.broadcast_to(mine, blocks.shape)
    return lax.all_to_all(spread, axes, 0, 0).reshape(rows, lanes)


def body(field, norm_gain, first_x, second_x, first_y, second_y, value_weight, out_weight):
    x_local, y_local, z_local, width = field.shape
    depth = width // H
    lanes = z_local * width
    total_x = x_local * lax.axis_size("row")
    total_y = y_local * lax.axis_size("col")
    slab_shape = (x_local, z_local, y_local, width)
    sum_y, normed = call(
        norm_kernel,
        [jax.ShapeDtypeStruct((y_local, width), F32), jax.ShapeDtypeStruct(slab_shape, BF16)],
        1 << 30,
        [
            pltpu.VMEM(slab_shape, BF16),
            pltpu.VMEM(slab_shape, BF16),
            pltpu.VMEM((1, width), F32),
            pltpu.VMEM((width, width), BF16),
            pltpu.SemaphoreType.DMA((2 * len(CUTS),)),
        ],
        out_specs=[pl.BlockSpec(memory_space=pltpu.VMEM), IN_HBM],
        limit=LIMIT_A,
        in_specs=[IN_HBM] * 3,
    )(jnp.transpose(field, (0, 2, 1, 3)), norm_gain.reshape(1, width), first_y)
    loaded = [
        pltpu.VMEM(slab_shape, BF16),
        pltpu.VMEM((width, width), BF16),
        pltpu.SemaphoreType.DMA((CHUNKS + 1,)),
    ]
    sum_x = call(
        sum_x_kernel, jax.ShapeDtypeStruct((x_local, width), F32), 1 << 30, loaded, limit=LIMIT_A, in_specs=[IN_HBM] * 2
    )(normed, first_x)
    value = call(
        value_kernel, jax.ShapeDtypeStruct((x_local, y_local, lanes), BF16), 1 << 30, loaded, in_specs=[IN_HBM] * 2
    )(normed, value_weight)
    sum_x, sum_y = pair_sums(sum_x, sum_y)
    mean_x = 0.5 / (total_y * z_local)
    mean_y = 0.5 / (total_x * z_local)
    part = call(
        functools.partial(outer_kernel, mean_x, mean_y),
        jax.ShapeDtypeStruct((depth * depth, lanes), BF16),
        1 << 30,
        [pltpu.VMEM((x_local, depth, lanes), F32), pltpu.VMEM((x_local, depth * width), F32)],
    )(sum_x, sum_y, second_x[:, width:], second_y[:, width:], value)
    total = total_sum(part)
    out = call(
        functools.partial(finish_kernel, mean_x * total_x**-0.5, mean_y * total_y**-0.5),
        jax.ShapeDtypeStruct(slab_shape, BF16),
        1 << 30,
        [
            pltpu.VMEM(slab_shape, BF16),
            pltpu.VMEM((depth * depth, lanes), F32),
            pltpu.VMEM((x_local, depth * width), F32),
            pltpu.SemaphoreType.DMA((x_local,)),
        ],
        out_specs=IN_HBM,
    )(sum_x, sum_y, second_x[:, :width], second_y[:, :width], total, out_weight)
    return jnp.transpose(out, (0, 2, 1, 3))


def solution(mesh):
    placed = (P("row", "col", "zs", None), P(), P(), P(), P(), P(), P(), P())
    return jax.shard_map(
        body, mesh=mesh, in_specs=placed, out_specs=P("row", "col", "zs", None), check_vma=False
    )
```

```python
import functools

import jax
import jax.numpy as jnp
from jax import lax
from jax.experimental import pallas as pl
from jax.experimental.pallas import tpu as pltpu
from jax.sharding import PartitionSpec as P

H = 8
EPS = 1e-05
HIGH = lax.Precision.HIGHEST
F32 = jnp.float32
BF16 = jnp.bfloat16
GELU_A = 0.7978845608028654
GELU_B = GELU_A * 0.044715
VMEM_LIMIT = 48 * 1024 * 1024
CHUNKS = 4
CUTS = (0, 2, 8, 14, 16)
GROUP = 8
LIMIT_A = 62 * 1024 * 1024
IN_HBM = pl.BlockSpec(memory_space=pltpu.HBM)


def dot(a, b):
    return jnp.dot(a, b, preferred_element_type=F32)


def halves(a):
    high = a.astype(BF16)
    return high, (a - high.astype(F32)).astype(BF16)


def summary(sums, scale, second):
    return jnp.dot(sums * scale, second.astype(F32), precision=HIGH)


def spread_into(ref, rows):
    width = rows.shape[1]
    depth = width // H
    start = lax.broadcasted_iota(jnp.int32, rows.shape, 1) // depth * depth
    for d in range(depth):
        ref[:, d * width : (d + 1) * width] = jnp.take_along_axis(rows, start + d, axis=1)


def gelu_twice(h):
    return h + h * jnp.tanh(h * (GELU_A + GELU_B * (h * h)))


def norm_kernel(field_hbm, gain_hbm, first_hbm, sum_y_ref, normed_hbm, field_ref, normed_ref, gain_ref, first_ref, sems):
    x_local, z_local, y_local, width = normed_ref.shape
    cuts = [x_local * k // 16 for k in CUTS]
    parts = [(a, b - a) for a, b in zip(cuts[:-1], cuts[1:])]
    count = len(parts)
    small = [
        pltpu.make_async_copy(gain_hbm, gain_ref, sems.at[2 * count]),
        pltpu.make_async_copy(first_hbm, first_ref, sems.at[2 * count + 1]),
    ]
    big = [
        pltpu.make_async_copy(field_hbm.at[pl.ds(a, n)], field_ref.at[pl.ds(a, n)], sems.at[c])
        for c, (a, n) in enumerate(parts)
    ]
    for copy in small + big:
        copy.start()
    for copy in small:
        copy.wait()
    gain = gain_ref[...]
    sum_y_ref[...] = jnp.zeros_like(sum_y_ref)
    outs = []

    for c, (a, n) in enumerate(parts):
        big[c].wait()
        part = pl.ds(a, n)
        values = field_ref[part].reshape(n * z_local * y_local, width).astype(F32)
        centred = values - jnp.mean(values, axis=-1, keepdims=True)
        spread = jnp.mean(centred * centred, axis=-1, keepdims=True)
        normed = (centred * lax.rsqrt(spread + EPS) * gain).astype(BF16)
        normed_ref[part] = normed.reshape(n, z_local, y_local, width)
        out = pltpu.make_async_copy(normed_ref.at[part], normed_hbm.at[part], sems.at[count + c])
        out.start()
        outs.append(out)
        g = gelu_twice(dot(normed, first_ref[...]))
        sum_y_ref[...] += jnp.sum(g.reshape(n * z_local, y_local, width), axis=0)
    for out in outs:
        out.wait()


def chunks_of(hbm, ref, sems):
    n = ref.shape[0] // CHUNKS
    copies = [
        pltpu.make_async_copy(hbm.at[pl.ds(c * n, n)], ref.at[pl.ds(c * n, n)], sems.at[c]) for c in range(CHUNKS)
    ]
    for copy in copies:
        copy.start()
    for c in range(CHUNKS):
        copies[c].wait()
        yield c * n, ref[pl.ds(c * n, n)].reshape(-1, ref.shape[3]), n


def sum_x_kernel(normed_hbm, first_hbm, sum_x_ref, normed_ref, first_ref, sems):
    load = pltpu.make_async_copy(first_hbm, first_ref, sems.at[CHUNKS])
    load.start()
    for start, rows, n in chunks_of(normed_hbm, normed_ref, sems):
        if start == 0:
            load.wait()
        g = gelu_twice(dot(rows, first_ref[...]))
        sum_x_ref[start : start + n, :] = jnp.sum(g.reshape(n, -1, g.shape[1]), axis=1)


def value_kernel(normed_hbm, weight_hbm, value_ref, normed_ref, weight_ref, sems):
    z_local, y_local, width = normed_ref.shape[1:]
    load = pltpu.make_async_copy(weight_hbm, weight_ref, sems.at[CHUNKS])
    load.start()
    for start, rows, n in chunks_of(normed_hbm, normed_ref, sems):
        if start == 0:
            load.wait()
        value = dot(rows, weight_ref[...]).astype(BF16).reshape(n, z_local, y_local, width)
        for z in range(z_local):
            value_ref[start : start + n, :, z * width : (z + 1) * width] = value[:, z]


def outer_kernel(scale_x, scale_y, sum_x_ref, sum_y_ref, key_x_ref, key_y_ref, value_ref, total_ref, part_ref, rows_ref):
    x_local, y_local, lanes = value_ref.shape
    width = key_x_ref.shape[0]
    depth = width // H
    key_y = summary(sum_y_ref[...], scale_y, key_y_ref[...])
    left = jnp.concatenate(halves(key_y.T), axis=1)
    spread_into(rows_ref, summary(sum_x_ref[...], scale_x, key_x_ref[...]))
    head = (lax.broadcasted_iota(jnp.int32, (depth, lanes), 1) % width) // depth

    def step(j, carry):
        group = [j * GROUP + q for q in range(GROUP)]
        fulls = [dot(left, jnp.concatenate([value_ref[i]] * 2, axis=0)) for i in group]
        for i, full in zip(group, fulls):
            acc = full[:depth]
            for h in range(1, H):
                acc = jnp.where(head == h, full[h * depth : (h + 1) * depth], acc)
            part_ref[i] = acc
        return carry

    lax.fori_loop(0, x_local // GROUP, step, 0)

    for z in range(lanes // width):
        cols = slice(z * width, (z + 1) * width)
        for d in range(depth):
            acc = jnp.zeros((depth, width), F32)
            for i in range(x_local):
                acc += rows_ref[i : i + 1, d * width : (d + 1) * width] * part_ref[i, :, cols]
            total_ref[d * depth : (d + 1) * depth, cols] = acc.astype(BF16)


def query_kernel(scale_x, scale_y, sum_x_ref, sum_y_ref, query_x_ref, query_y_ref, left_ref, rows_ref):
    high, low = halves(summary(sum_y_ref[...], scale_y, query_y_ref[...]))
    left_ref[...] = jnp.concatenate(
        [jnp.concatenate([high, high], axis=1), jnp.concatenate([low, jnp.zeros_like(low)], axis=1)], axis=0
    )
    spread_into(rows_ref, summary(sum_x_ref[...], scale_x, query_x_ref[...]))


def finish_kernel(left_ref, rows_ref, total_ref, weight_ref, out_hbm, out_ref, wide_ref, sems):
    x_local, z_local, y_local, width = out_ref.shape
    depth = width // H
    lanes = z_local * width
    wide_ref[...] = total_ref[...].astype(F32)
    left = left_ref[...]
    head = (lax.broadcasted_iota(jnp.int32, (depth, lanes), 1) % width) // depth
    zero = jnp.zeros((depth, lanes), BF16)

    def copy_of(i):
        return pltpu.make_async_copy(out_ref.at[i], out_hbm.at[i], sems.at[i])

    def right_of(i):
        pieces = []
        rows = rows_ref[pl.ds(i, 1), :]
        for z in range(z_local):
            cols = slice(z * width, (z + 1) * width)
            acc = jnp.zeros((depth, width), F32)
            for d in range(depth):
                acc += rows[:, d * width : (d + 1) * width] * wide_ref[d * depth : (d + 1) * depth, cols]
            pieces.append(acc)
        return jnp.concatenate(
            [jnp.where(head == h, w, zero) for w in halves(jnp.concatenate(pieces, axis=1)) for h in range(H)],
            axis=0,
        )

    def step(j, carry):
        group = [j * GROUP + q for q in range(GROUP)]
        boths = [dot(left, right) for right in [right_of(i) for i in group]]
        for i, both in zip(group, boths):
            u = (both[:y_local] + both[y_local:]).astype(BF16)
            u = jnp.concatenate([u[:, z * width : (z + 1) * width] for z in range(z_local)], axis=0)
            out_ref[i] = dot(u, weight_ref[...]).astype(BF16).reshape(z_local, y_local, width)
            copy_of(i).start()
        return carry

    lax.fori_loop(0, x_local // GROUP, step, 0)

    def finish(i, carry):
        copy_of(i).wait()
        return carry

    lax.fori_loop(0, x_local, finish, 0)


def call(kernel, out_shape, flops, scratch=(), limit=VMEM_LIMIT, **specs):
    return pl.pallas_call(
        kernel,
        out_shape=out_shape,
        scratch_shapes=list(scratch),
        compiler_params=pltpu.CompilerParams(vmem_limit_bytes=limit),
        cost_estimate=pl.CostEstimate(flops=flops, bytes_accessed=4 << 20, transcendentals=0),
        **specs,
    )


def sum_over(value, axis, stride, radix):
    total = value
    for k in range(1, radix):
        pairs = []
        for i in range(lax.axis_size(axis)):
            digit = i // stride % radix
            pairs.append((i, i + ((digit + k) % radix - digit) * stride))
        total = total + lax.ppermute(value, axis, pairs)
    return total


def digits(size):
    steps = []
    while size > 1:
        radix = 2 if size == 2 else 4
        size //= radix
        steps.append((size, radix))
    return steps


def sums_over(value, axis):
    for step in digits(lax.axis_size(axis)):
        value = sum_over(value, axis, *step)
    return value


def total_sum(part, beside, *args):
    axes = ("row", "col")
    rows_n, cols_n = lax.axis_size("row"), lax.axis_size("col")
    half = rows_n // 2
    n = half * cols_n
    groups = [[(k * half + r) * cols_n + c for r in range(half) for c in range(cols_n)] for k in range(2)]
    rows, lanes = part.shape
    blocks = lax.all_to_all(part.reshape(n, rows // n, lanes), axes, 0, 0, axis_index_groups=groups)
    mine = jnp.sum(blocks.astype(F32), axis=0)
    swap = [(r, (r + half) % rows_n) for r in range(rows_n)]
    mine, args = lax.optimization_barrier((mine, args))
    other = lax.ppermute(mine.astype(BF16), "row", swap)
    done = beside(*args)
    mine, done = lax.optimization_barrier(((mine + other.astype(F32)).astype(BF16), done))
    spread = jnp.broadcast_to(mine, blocks.shape)
    return lax.all_to_all(spread, axes, 0, 0, axis_index_groups=groups).reshape(rows, lanes), done


def body(field, norm_gain, first_x, second_x, first_y, second_y, value_weight, out_weight):
    x_local, y_local, z_local, width = field.shape
    depth = width // H
    lanes = z_local * width
    total_x = x_local * lax.axis_size("row")
    total_y = y_local * lax.axis_size("col")
    slab_shape = (x_local, z_local, y_local, width)
    sum_y, normed = call(
        norm_kernel,
        [jax.ShapeDtypeStruct((y_local, width), F32), jax.ShapeDtypeStruct(slab_shape, BF16)],
        1 << 30,
        [
            pltpu.VMEM(slab_shape, BF16),
            pltpu.VMEM(slab_shape, BF16),
            pltpu.VMEM((1, width), F32),
            pltpu.VMEM((width, width), BF16),
            pltpu.SemaphoreType.DMA((2 * len(CUTS),)),
        ],
        out_specs=[pl.BlockSpec(memory_space=pltpu.VMEM), IN_HBM],
        limit=LIMIT_A,
        in_specs=[IN_HBM] * 3,
    )(jnp.transpose(field, (0, 2, 1, 3)), norm_gain.reshape(1, width), first_y)
    loaded = [
        pltpu.VMEM(slab_shape, BF16),
        pltpu.VMEM((width, width), BF16),
        pltpu.SemaphoreType.DMA((CHUNKS + 1,)),
    ]
    sum_x = call(
        sum_x_kernel, jax.ShapeDtypeStruct((x_local, width), F32), 1 << 30, loaded, limit=LIMIT_A, in_specs=[IN_HBM] * 2
    )(normed, first_x)
    value = call(
        value_kernel, jax.ShapeDtypeStruct((x_local, y_local, lanes), BF16), 1 << 30, loaded, in_specs=[IN_HBM] * 2
    )(normed, value_weight)
    sum_x = sums_over(sum_x, "col")
    sum_y = sums_over(sum_y, "row")
    mean_x = 0.5 / (total_y * z_local)
    mean_y = 0.5 / (total_x * z_local)
    part = call(
        functools.partial(outer_kernel, mean_x, mean_y),
        jax.ShapeDtypeStruct((depth * depth, lanes), BF16),
        1 << 30,
        [pltpu.VMEM((x_local, depth, lanes), F32), pltpu.VMEM((x_local, depth * width), F32)],
    )(sum_x, sum_y, second_x[:, width:], second_y[:, width:], value)
    queries = call(
        functools.partial(query_kernel, mean_x * total_x**-0.5, mean_y * total_y**-0.5),
        [
            jax.ShapeDtypeStruct((2 * y_local, 2 * width), BF16),
            jax.ShapeDtypeStruct((x_local, depth * width), F32),
        ],
        1 << 30,
    )
    total, (left, rows) = total_sum(part, queries, sum_x, sum_y, second_x[:, :width], second_y[:, :width])
    out = call(
        finish_kernel,
        jax.ShapeDtypeStruct(slab_shape, BF16),
        1 << 30,
        [
            pltpu.VMEM(slab_shape, BF16),
            pltpu.VMEM((depth * depth, lanes), F32),
            pltpu.SemaphoreType.DMA((x_local,)),
        ],
        out_specs=IN_HBM,
    )(left, rows, total, out_weight)
    return jnp.transpose(out, (0, 2, 1, 3))


def solution(mesh):
    placed = (P("row", "col", "zs", None), P(), P(), P(), P(), P(), P(), P())
    return jax.shard_map(
        body, mesh=mesh, in_specs=placed, out_specs=P("row", "col", "zs", None), check_vma=False
    )
```

```python
import functools

import jax
import jax.numpy as jnp
from jax import lax
from jax.experimental import pallas as pl
from jax.experimental.pallas import tpu as pltpu
from jax.sharding import PartitionSpec as P

H = 8
EPS = 1e-05
HIGH = lax.Precision.HIGHEST
F32 = jnp.float32
BF16 = jnp.bfloat16
GELU_A = 0.7978845608028654
GELU_B = GELU_A * 0.044715
VMEM_LIMIT = 48 * 1024 * 1024
CHUNKS = 4
CUTS = (0, 2, 8, 14, 16)
GROUP = 8
LIMIT_A = 62 * 1024 * 1024
IN_HBM = pl.BlockSpec(memory_space=pltpu.HBM)


def dot(a, b):
    return jnp.dot(a, b, preferred_element_type=F32)


def halves(a):
    high = a.astype(BF16)
    return high, (a - high.astype(F32)).astype(BF16)


def summary(sums, scale, second):
    return jnp.dot(sums * scale, second.astype(F32), precision=HIGH)


def spread_into(ref, rows):
    width = rows.shape[1]
    depth = width // H
    start = lax.broadcasted_iota(jnp.int32, rows.shape, 1) // depth * depth
    for d in range(depth):
        ref[:, d * width : (d + 1) * width] = jnp.take_along_axis(rows, start + d, axis=1)


def gelu_twice(h):
    return h + h * jnp.tanh(h * (GELU_A + GELU_B * (h * h)))


def norm_kernel(field_hbm, gain_hbm, first_hbm, sum_y_ref, normed_hbm, field_ref, normed_ref, gain_ref, first_ref, sems):
    x_local, z_local, y_local, width = normed_ref.shape
    cuts = [x_local * k // 16 for k in CUTS]
    parts = [(a, b - a) for a, b in zip(cuts[:-1], cuts[1:])]
    count = len(parts)
    small = [
        pltpu.make_async_copy(gain_hbm, gain_ref, sems.at[2 * count]),
        pltpu.make_async_copy(first_hbm, first_ref, sems.at[2 * count + 1]),
    ]
    big = [
        pltpu.make_async_copy(field_hbm.at[pl.ds(a, n)], field_ref.at[pl.ds(a, n)], sems.at[c])
        for c, (a, n) in enumerate(parts)
    ]
    for copy in big[:1] + small + big[1:]:
        copy.start()
    total = jnp.zeros(sum_y_ref.shape, F32)
    outs = []

    for c, (a, n) in enumerate(parts):
        big[c].wait()
        part = pl.ds(a, n)
        values = field_ref[part].reshape(n * z_local * y_local, width).astype(F32)
        centred = values - jnp.mean(values, axis=-1, keepdims=True)
        spread = jnp.mean(centred * centred, axis=-1, keepdims=True)
        if c == 0:
            for copy in small:
                copy.wait()
        normed = (centred * lax.rsqrt(spread + EPS) * gain_ref[...]).astype(BF16)
        normed_ref[part] = normed.reshape(n, z_local, y_local, width)
        out = pltpu.make_async_copy(normed_ref.at[part], normed_hbm.at[part], sems.at[count + c])
        out.start()
        outs.append(out)
        g = gelu_twice(dot(normed, first_ref[...]))
        total += jnp.sum(g.reshape(n * z_local, y_local, width), axis=0)
    sum_y_ref[...] = total
    for out in outs:
        out.wait()


def chunks_of(ref):
    n = ref.shape[0] // CHUNKS
    for c in range(CHUNKS):
        yield c * n, ref[pl.ds(c * n, n)].reshape(-1, ref.shape[3]), n


def sum_x_kernel(normed_ref, first_ref, sum_x_ref):
    for start, rows, n in chunks_of(normed_ref):
        g = gelu_twice(dot(rows, first_ref[...]))
        sum_x_ref[start : start + n, :] = jnp.sum(g.reshape(n, -1, g.shape[1]), axis=1)


def value_kernel(normed_ref, weight_ref, value_ref):
    z_local, y_local, width = normed_ref.shape[1:]
    for start, rows, n in chunks_of(normed_ref):
        value = dot(rows, weight_ref[...]).astype(BF16).reshape(n, z_local, y_local, width)
        for z in range(z_local):
            value_ref[start : start + n, :, z * width : (z + 1) * width] = value[:, z]


def outer_kernel(scale_x, scale_y, sum_x_ref, sum_y_ref, key_x_ref, key_y_ref, value_ref, total_ref, part_ref, rows_ref):
    x_local, y_local, lanes = value_ref.shape
    width = key_x_ref.shape[0]
    depth = width // H
    key_y = summary(sum_y_ref[...], scale_y, key_y_ref[...])
    left = jnp.concatenate(halves(key_y.T), axis=1)
    spread_into(rows_ref, summary(sum_x_ref[...], scale_x, key_x_ref[...]))
    head = (lax.broadcasted_iota(jnp.int32, (depth, lanes), 1) % width) // depth

    def step(j, carry):
        group = [j * GROUP + q for q in range(GROUP)]
        fulls = [dot(left, jnp.concatenate([value_ref[i]] * 2, axis=0)) for i in group]
        for i, full in zip(group, fulls):
            acc = full[:depth]
            for h in range(1, H):
                acc = jnp.where(head == h, full[h * depth : (h + 1) * depth], acc)
            part_ref[i] = acc
        return carry

    lax.fori_loop(0, x_local // GROUP, step, 0)

    for z in range(lanes // width):
        cols = slice(z * width, (z + 1) * width)
        for d in range(depth):
            acc = jnp.zeros((depth, width), F32)
            for i in range(x_local):
                acc += rows_ref[i : i + 1, d * width : (d + 1) * width] * part_ref[i, :, cols]
            total_ref[d * depth : (d + 1) * depth, cols] = acc.astype(BF16)


def query_kernel(scale_x, scale_y, sum_x_ref, sum_y_ref, query_x_ref, query_y_ref, left_ref, rows_ref):
    high, low = halves(summary(sum_y_ref[...], scale_y, query_y_ref[...]))
    left_ref[...] = jnp.concatenate(
        [jnp.concatenate([high, high], axis=1), jnp.concatenate([low, jnp.zeros_like(low)], axis=1)], axis=0
    )
    spread_into(rows_ref, summary(sum_x_ref[...], scale_x, query_x_ref[...]))


def finish_kernel(left_ref, rows_ref, total_ref, weight_ref, out_hbm, out_ref, wide_ref, sems):
    x_local, z_local, y_local, width = out_ref.shape
    depth = width // H
    lanes = z_local * width
    wide_ref[...] = total_ref[...].astype(F32)
    left = left_ref[...]
    head = (lax.broadcasted_iota(jnp.int32, (depth, lanes), 1) % width) // depth
    zero = jnp.zeros((depth, lanes), BF16)

    def copy_of(i):
        return pltpu.make_async_copy(out_ref.at[i], out_hbm.at[i], sems.at[i])

    def right_of(i):
        pieces = []
        rows = rows_ref[pl.ds(i, 1), :]
        for z in range(z_local):
            cols = slice(z * width, (z + 1) * width)
            acc = jnp.zeros((depth, width), F32)
            for d in range(depth):
                acc += rows[:, d * width : (d + 1) * width] * wide_ref[d * depth : (d + 1) * depth, cols]
            pieces.append(acc)
        return jnp.concatenate(
            [jnp.where(head == h, w, zero) for w in halves(jnp.concatenate(pieces, axis=1)) for h in range(H)],
            axis=0,
        )

    def step(j, carry):
        group = [j * GROUP + q for q in range(GROUP)]
        boths = [dot(left, right) for right in [right_of(i) for i in group]]
        for i, both in zip(group, boths):
            u = (both[:y_local] + both[y_local:]).astype(BF16)
            u = jnp.concatenate([u[:, z * width : (z + 1) * width] for z in range(z_local)], axis=0)
            out_ref[i] = dot(u, weight_ref[...]).astype(BF16).reshape(z_local, y_local, width)
            copy_of(i).start()
        return carry

    lax.fori_loop(0, x_local // GROUP, step, 0)

    def finish(i, carry):
        copy_of(i).wait()
        return carry

    lax.fori_loop(0, x_local, finish, 0)


def call(kernel, out_shape, flops, scratch=(), limit=VMEM_LIMIT, **specs):
    return pl.pallas_call(
        kernel,
        out_shape=out_shape,
        scratch_shapes=list(scratch),
        compiler_params=pltpu.CompilerParams(vmem_limit_bytes=limit),
        cost_estimate=pl.CostEstimate(flops=flops, bytes_accessed=4 << 20, transcendentals=0),
        **specs,
    )


def sum_over(value, axis, stride, radix):
    total = value
    for k in range(1, radix):
        pairs = []
        for i in range(lax.axis_size(axis)):
            digit = i // stride % radix
            pairs.append((i, i + ((digit + k) % radix - digit) * stride))
        total = total + lax.ppermute(value, axis, pairs)
    return total


def digits(size):
    steps = []
    while size > 1:
        radix = 2 if size == 2 else 4
        size //= radix
        steps.append((size, radix))
    return steps


def sums_over(value, axis):
    for step in digits(lax.axis_size(axis)):
        value = sum_over(value, axis, *step)
    return value


def total_sum(part, beside, *args):
    axes = ("row", "col")
    rows_n, cols_n = lax.axis_size("row"), lax.axis_size("col")
    half = rows_n // 2
    n = half * cols_n
    groups = [[(k * half + r) * cols_n + c for r in range(half) for c in range(cols_n)] for k in range(2)]
    rows, lanes = part.shape
    blocks = lax.all_to_all(part.reshape(n, rows // n, lanes), axes, 0, 0, axis_index_groups=groups)
    mine = jnp.sum(blocks.astype(F32), axis=0)
    swap = [(r, (r + half) % rows_n) for r in range(rows_n)]
    mine, args = lax.optimization_barrier((mine, args))
    other = lax.ppermute(mine.astype(BF16), "row", swap)
    done = beside(*args)
    mine, done = lax.optimization_barrier(((mine + other.astype(F32)).astype(BF16), done))
    spread = jnp.broadcast_to(mine, blocks.shape)
    return lax.all_to_all(spread, axes, 0, 0, axis_index_groups=groups).reshape(rows, lanes), done


def body(field, norm_gain, first_x, second_x, first_y, second_y, value_weight, out_weight):
    x_local, y_local, z_local, width = field.shape
    depth = width // H
    lanes = z_local * width
    total_x = x_local * lax.axis_size("row")
    total_y = y_local * lax.axis_size("col")
    slab_shape = (x_local, z_local, y_local, width)
    sum_y, normed = call(
        norm_kernel,
        [jax.ShapeDtypeStruct((y_local, width), F32), jax.ShapeDtypeStruct(slab_shape, BF16)],
        1 << 30,
        [
            pltpu.VMEM(slab_shape, BF16),
            pltpu.VMEM(slab_shape, BF16),
            pltpu.VMEM((1, width), F32),
            pltpu.VMEM((width, width), BF16),
            pltpu.SemaphoreType.DMA((2 * len(CUTS),)),
        ],
        out_specs=[pl.BlockSpec(memory_space=pltpu.VMEM), IN_HBM],
        limit=LIMIT_A,
        in_specs=[IN_HBM] * 3,
    )(jnp.transpose(field, (0, 2, 1, 3)), norm_gain.reshape(1, width), first_y)
    sum_x = call(sum_x_kernel, jax.ShapeDtypeStruct((x_local, width), F32), 1 << 30)(normed, first_x)
    value = call(value_kernel, jax.ShapeDtypeStruct((x_local, y_local, lanes), BF16), 1 << 30)(normed, value_weight)
    sum_x = sums_over(sum_x, "col")
    sum_y = sums_over(sum_y, "row")
    mean_x = 0.5 / (total_y * z_local)
    mean_y = 0.5 / (total_x * z_local)
    part = call(
        functools.partial(outer_kernel, mean_x, mean_y),
        jax.ShapeDtypeStruct((depth * depth, lanes), BF16),
        1 << 30,
        [pltpu.VMEM((x_local, depth, lanes), F32), pltpu.VMEM((x_local, depth * width), F32)],
    )(sum_x, sum_y, second_x[:, width:], second_y[:, width:], value)
    queries = call(
        functools.partial(query_kernel, mean_x * total_x**-0.5, mean_y * total_y**-0.5),
        [
            jax.ShapeDtypeStruct((2 * y_local, 2 * width), BF16),
            jax.ShapeDtypeStruct((x_local, depth * width), F32),
        ],
        1 << 30,
    )
    total, (left, rows) = total_sum(part, queries, sum_x, sum_y, second_x[:, :width], second_y[:, :width])
    out = call(
        finish_kernel,
        jax.ShapeDtypeStruct(slab_shape, BF16),
        1 << 30,
        [
            pltpu.VMEM(slab_shape, BF16),
            pltpu.VMEM((depth * depth, lanes), F32),
            pltpu.SemaphoreType.DMA((x_local,)),
        ],
        out_specs=IN_HBM,
    )(left, rows, total, out_weight)
    return jnp.transpose(out, (0, 2, 1, 3))


def solution(mesh):
    placed = (P("row", "col", "zs", None), P(), P(), P(), P(), P(), P(), P())
    return jax.shard_map(
        body, mesh=mesh, in_specs=placed, out_specs=P("row", "col", "zs", None), check_vma=False
    )
```

```python
import functools

import jax
import jax.numpy as jnp
from jax import lax
from jax.experimental import pallas as pl
from jax.experimental.pallas import tpu as pltpu
from jax.sharding import PartitionSpec as P

H = 8
EPS = 1e-05
F32 = jnp.float32
BF16 = jnp.bfloat16
GELU_A = 0.7978845608028654
GELU_B = GELU_A * 0.044715
VMEM_LIMIT = 48 * 1024 * 1024
CHUNKS = 4
CUTS = (0, 2, 8, 14, 16)
GROUP = 8
LIMIT_A = 62 * 1024 * 1024
IN_HBM = pl.BlockSpec(memory_space=pltpu.HBM)


def dot(a, b):
    return jnp.dot(a, b, preferred_element_type=F32)


def halves(a):
    high = a.astype(BF16)
    return high, (a - high.astype(F32)).astype(BF16)


def summary(sums, scale, second):
    return dot(jnp.concatenate(halves(sums * scale), axis=1), jnp.concatenate([second, second], axis=0))


def spread_into(ref, rows):
    width = rows.shape[1]
    depth = width // H
    start = lax.broadcasted_iota(jnp.int32, rows.shape, 1) // depth * depth
    for d in range(depth):
        ref[:, d * width : (d + 1) * width] = jnp.take_along_axis(rows, start + d, axis=1)


def gelu_twice(h):
    return h + h * jnp.tanh(h * (GELU_A + GELU_B * (h * h)))


def norm_kernel(field_hbm, gain_hbm, first_hbm, sum_y_ref, normed_hbm, field_ref, normed_ref, gain_ref, first_ref, sems):
    x_local, z_local, y_local, width = normed_ref.shape
    cuts = [x_local * k // 16 for k in CUTS]
    parts = [(a, b - a) for a, b in zip(cuts[:-1], cuts[1:])]
    count = len(parts)
    small = [
        pltpu.make_async_copy(gain_hbm, gain_ref, sems.at[2 * count]),
        pltpu.make_async_copy(first_hbm, first_ref, sems.at[2 * count + 1]),
    ]
    big = [
        pltpu.make_async_copy(field_hbm.at[pl.ds(a, n)], field_ref.at[pl.ds(a, n)], sems.at[c])
        for c, (a, n) in enumerate(parts)
    ]
    for copy in big[:1] + small + big[1:]:
        copy.start()
    total = jnp.zeros(sum_y_ref.shape, F32)
    ones = jnp.full((width, width), 1.0 / width, BF16)
    outs = []

    for c, (a, n) in enumerate(parts):
        big[c].wait()
        part = pl.ds(a, n)
        values = field_ref[part].reshape(n * z_local * y_local, width)
        centred = values.astype(F32) - dot(values, ones)
        spread = jnp.mean(centred * centred, axis=-1, keepdims=True)
        if c == 0:
            for copy in small:
                copy.wait()
        normed = (centred * lax.rsqrt(spread + EPS) * gain_ref[...]).astype(BF16)
        normed_ref[part] = normed.reshape(n, z_local, y_local, width)
        out = pltpu.make_async_copy(normed_ref.at[part], normed_hbm.at[part], sems.at[count + c])
        out.start()
        outs.append(out)
        g = gelu_twice(dot(normed, first_ref[...]))
        total += jnp.sum(g.reshape(n * z_local, y_local, width), axis=0)
    sum_y_ref[...] = total
    for out in outs:
        out.wait()


def chunks_of(ref):
    n = ref.shape[0] // CHUNKS
    for c in range(CHUNKS):
        yield c * n, ref[pl.ds(c * n, n)].reshape(-1, ref.shape[3]), n


def sum_x_kernel(normed_ref, first_ref, sum_x_ref):
    for start, rows, n in chunks_of(normed_ref):
        g = gelu_twice(dot(rows, first_ref[...]))
        sum_x_ref[start : start + n, :] = jnp.sum(g.reshape(n, -1, g.shape[1]), axis=1)


def value_kernel(normed_ref, weight_ref, value_ref):
    z_local, y_local, width = normed_ref.shape[1:]
    for start, rows, n in chunks_of(normed_ref):
        value = dot(rows, weight_ref[...]).astype(BF16).reshape(n, z_local, y_local, width)
        for z in range(z_local):
            value_ref[start : start + n, :, z * width : (z + 1) * width] = value[:, z]


def outer_kernel(scale_x, scale_y, sum_x_ref, sum_y_ref, key_x_ref, key_y_ref, value_ref, total_ref, part_ref, rows_ref):
    x_local, y_local, lanes = value_ref.shape
    width = key_x_ref.shape[0]
    depth = width // H
    key_y = summary(sum_y_ref[...], scale_y, key_y_ref[...])
    left = jnp.concatenate(halves(key_y.T), axis=1)
    spread_into(rows_ref, summary(sum_x_ref[...], scale_x, key_x_ref[...]))
    head = (lax.broadcasted_iota(jnp.int32, (depth, lanes), 1) % width) // depth

    def step(j, carry):
        group = [j * GROUP + q for q in range(GROUP)]
        fulls = [dot(left, jnp.concatenate([value_ref[i]] * 2, axis=0)) for i in group]
        for i, full in zip(group, fulls):
            acc = full[:depth]
            for h in range(1, H):
                acc = jnp.where(head == h, full[h * depth : (h + 1) * depth], acc)
            part_ref[i] = acc
        return carry

    lax.fori_loop(0, x_local // GROUP, step, 0)

    for z in range(lanes // width):
        cols = slice(z * width, (z + 1) * width)
        for d in range(depth):
            acc = jnp.zeros((depth, width), F32)
            for i in range(x_local):
                acc += rows_ref[i : i + 1, d * width : (d + 1) * width] * part_ref[i, :, cols]
            total_ref[d * depth : (d + 1) * depth, cols] = acc.astype(BF16)


def query_kernel(scale_x, scale_y, sum_x_ref, sum_y_ref, query_x_ref, query_y_ref, left_ref, rows_ref):
    high, low = halves(summary(sum_y_ref[...], scale_y, query_y_ref[...]))
    left_ref[...] = jnp.concatenate(
        [jnp.concatenate([high, high], axis=1), jnp.concatenate([low, jnp.zeros_like(low)], axis=1)], axis=0
    )
    spread_into(rows_ref, summary(sum_x_ref[...], scale_x, query_x_ref[...]))


def finish_kernel(left_ref, rows_ref, total_ref, weight_ref, out_hbm, out_ref, wide_ref, sems):
    x_local, z_local, y_local, width = out_ref.shape
    depth = width // H
    lanes = z_local * width
    wide_ref[...] = total_ref[...].astype(F32)
    left = left_ref[...]
    head = (lax.broadcasted_iota(jnp.int32, (depth, lanes), 1) % width) // depth
    zero = jnp.zeros((depth, lanes), BF16)

    def copy_of(i):
        return pltpu.make_async_copy(out_ref.at[i], out_hbm.at[i], sems.at[i])

    def right_of(i):
        pieces = []
        rows = rows_ref[pl.ds(i, 1), :]
        for z in range(z_local):
            cols = slice(z * width, (z + 1) * width)
            acc = jnp.zeros((depth, width), F32)
            for d in range(depth):
                acc += rows[:, d * width : (d + 1) * width] * wide_ref[d * depth : (d + 1) * depth, cols]
            pieces.append(acc)
        return jnp.concatenate(
            [jnp.where(head == h, w, zero) for w in halves(jnp.concatenate(pieces, axis=1)) for h in range(H)],
            axis=0,
        )

    def step(j, carry):
        group = [j * GROUP + q for q in range(GROUP)]
        boths = [dot(left, right) for right in [right_of(i) for i in group]]
        for i, both in zip(group, boths):
            u = (both[:y_local] + both[y_local:]).astype(BF16)
            u = jnp.concatenate([u[:, z * width : (z + 1) * width] for z in range(z_local)], axis=0)
            out_ref[i] = dot(u, weight_ref[...]).astype(BF16).reshape(z_local, y_local, width)
            copy_of(i).start()
        return carry

    lax.fori_loop(0, x_local // GROUP, step, 0)

    def finish(i, carry):
        copy_of(i).wait()
        return carry

    lax.fori_loop(0, x_local, finish, 0)


def call(kernel, out_shape, flops, scratch=(), limit=VMEM_LIMIT, **specs):
    return pl.pallas_call(
        kernel,
        out_shape=out_shape,
        scratch_shapes=list(scratch),
        compiler_params=pltpu.CompilerParams(vmem_limit_bytes=limit),
        cost_estimate=pl.CostEstimate(flops=flops, bytes_accessed=4 << 20, transcendentals=0),
        **specs,
    )


def sum_over(value, axis, stride, radix):
    total = value
    for k in range(1, radix):
        pairs = []
        for i in range(lax.axis_size(axis)):
            digit = i // stride % radix
            pairs.append((i, i + ((digit + k) % radix - digit) * stride))
        total = total + lax.ppermute(value, axis, pairs)
    return total


def digits(size):
    steps = []
    while size > 1:
        radix = 2 if size == 2 else 4
        size //= radix
        steps.append((size, radix))
    return steps


def sums_over(value, axis):
    for step in digits(lax.axis_size(axis)):
        value = sum_over(value, axis, *step)
    return value


def total_sum(part, beside, *args):
    axes = ("row", "col")
    rows_n, cols_n = lax.axis_size("row"), lax.axis_size("col")
    half = rows_n // 2
    n = half * cols_n
    groups = [[(k * half + r) * cols_n + c for r in range(half) for c in range(cols_n)] for k in range(2)]
    rows, lanes = part.shape
    blocks = lax.all_to_all(part.reshape(n, rows // n, lanes), axes, 0, 0, axis_index_groups=groups)
    mine = jnp.sum(blocks.astype(F32), axis=0)
    swap = [(r, (r + half) % rows_n) for r in range(rows_n)]
    mine, args = lax.optimization_barrier((mine, args))
    other = lax.ppermute(mine.astype(BF16), "row", swap)
    done = beside(*args)
    mine, done = lax.optimization_barrier(((mine + other.astype(F32)).astype(BF16), done))
    spread = jnp.broadcast_to(mine, blocks.shape)
    return lax.all_to_all(spread, axes, 0, 0, axis_index_groups=groups).reshape(rows, lanes), done


def body(field, norm_gain, first_x, second_x, first_y, second_y, value_weight, out_weight):
    x_local, y_local, z_local, width = field.shape
    depth = width // H
    lanes = z_local * width
    total_x = x_local * lax.axis_size("row")
    total_y = y_local * lax.axis_size("col")
    slab_shape = (x_local, z_local, y_local, width)
    sum_y, normed = call(
        norm_kernel,
        [jax.ShapeDtypeStruct((y_local, width), F32), jax.ShapeDtypeStruct(slab_shape, BF16)],
        1 << 30,
        [
            pltpu.VMEM(slab_shape, BF16),
            pltpu.VMEM(slab_shape, BF16),
            pltpu.VMEM((1, width), F32),
            pltpu.VMEM((width, width), BF16),
            pltpu.SemaphoreType.DMA((2 * len(CUTS),)),
        ],
        out_specs=[pl.BlockSpec(memory_space=pltpu.VMEM), IN_HBM],
        limit=LIMIT_A,
        in_specs=[IN_HBM] * 3,
    )(jnp.transpose(field, (0, 2, 1, 3)), norm_gain.reshape(1, width), first_y)
    sum_x = call(sum_x_kernel, jax.ShapeDtypeStruct((x_local, width), F32), 1 << 30)(normed, first_x)
    value = call(value_kernel, jax.ShapeDtypeStruct((x_local, y_local, lanes), BF16), 1 << 30)(normed, value_weight)
    sum_x = sums_over(sum_x, "col")
    sum_y = sums_over(sum_y, "row")
    mean_x = 0.5 / (total_y * z_local)
    mean_y = 0.5 / (total_x * z_local)
    part = call(
        functools.partial(outer_kernel, mean_x, mean_y),
        jax.ShapeDtypeStruct((depth * depth, lanes), BF16),
        1 << 30,
        [pltpu.VMEM((x_local, depth, lanes), F32), pltpu.VMEM((x_local, depth * width), F32)],
    )(sum_x, sum_y, second_x[:, width:], second_y[:, width:], value)
    queries = call(
        functools.partial(query_kernel, mean_x * total_x**-0.5, mean_y * total_y**-0.5),
        [
            jax.ShapeDtypeStruct((2 * y_local, 2 * width), BF16),
            jax.ShapeDtypeStruct((x_local, depth * width), F32),
        ],
        1 << 30,
    )
    total, (left, rows) = total_sum(part, queries, sum_x, sum_y, second_x[:, :width], second_y[:, :width])
    out = call(
        finish_kernel,
        jax.ShapeDtypeStruct(slab_shape, BF16),
        1 << 30,
        [
            pltpu.VMEM(slab_shape, BF16),
            pltpu.VMEM((depth * depth, lanes), F32),
            pltpu.SemaphoreType.DMA((x_local,)),
        ],
        out_specs=IN_HBM,
    )(left, rows, total, out_weight)
    return jnp.transpose(out, (0, 2, 1, 3))


def solution(mesh):
    placed = (P("row", "col", "zs", None), P(), P(), P(), P(), P(), P(), P())
    return jax.shard_map(
        body, mesh=mesh, in_specs=placed, out_specs=P("row", "col", "zs", None), check_vma=False
    )
```

```python
import functools

import jax
import jax.numpy as jnp
from jax import lax
from jax.experimental import pallas as pl
from jax.experimental.pallas import tpu as pltpu
from jax.sharding import PartitionSpec as P

H = 8
EPS = 1e-05
F32 = jnp.float32
BF16 = jnp.bfloat16
GELU_A = 0.7978845608028654
GELU_B = GELU_A * 0.044715
VMEM_LIMIT = 48 * 1024 * 1024
CHUNKS = 4
CUTS = (0, 2, 8, 14, 16)
GROUP = 8
WIDE_GROUP = 16
LIMIT_A = 62 * 1024 * 1024
IN_HBM = pl.BlockSpec(memory_space=pltpu.HBM)


def dot(a, b):
    return jnp.dot(a, b, preferred_element_type=F32)


def halves(a):
    high = a.astype(BF16)
    return high, (a - high.astype(F32)).astype(BF16)


def summary(sums, scale, second):
    return dot(jnp.concatenate(halves(sums * scale), axis=1), jnp.concatenate([second, second], axis=0))


def spread_into(ref, rows):
    width = rows.shape[1]
    depth = width // H
    start = lax.broadcasted_iota(jnp.int32, rows.shape, 1) // depth * depth
    for d in range(depth):
        ref[:, d * width : (d + 1) * width] = jnp.take_along_axis(rows, start + d, axis=1)


def gelu_twice(h):
    return h + h * jnp.tanh(h * (GELU_A + GELU_B * (h * h)))


def norm_kernel(field_hbm, gain_hbm, first_hbm, sum_y_ref, normed_hbm, field_ref, normed_ref, gain_ref, first_ref, sems):
    x_local, z_local, y_local, width = normed_ref.shape
    cuts = [x_local * k // 16 for k in CUTS]
    parts = [(a, b - a) for a, b in zip(cuts[:-1], cuts[1:])]
    count = len(parts)
    small = [
        pltpu.make_async_copy(gain_hbm, gain_ref, sems.at[2 * count]),
        pltpu.make_async_copy(first_hbm, first_ref, sems.at[2 * count + 1]),
    ]
    big = [
        pltpu.make_async_copy(field_hbm.at[pl.ds(a, n)], field_ref.at[pl.ds(a, n)], sems.at[c])
        for c, (a, n) in enumerate(parts)
    ]
    for copy in big[:1] + small + big[1:]:
        copy.start()
    total = jnp.zeros(sum_y_ref.shape, F32)
    ones = jnp.full((width, width), 1.0 / width, BF16)
    outs = []

    for c, (a, n) in enumerate(parts):
        big[c].wait()
        part = pl.ds(a, n)
        values = field_ref[part].reshape(n * z_local * y_local, width)
        centred = values.astype(F32) - dot(values, ones)
        spread = jnp.mean(centred * centred, axis=-1, keepdims=True)
        if c == 0:
            for copy in small:
                copy.wait()
        normed = (centred * lax.rsqrt(spread + EPS) * gain_ref[...]).astype(BF16)
        normed_ref[part] = normed.reshape(n, z_local, y_local, width)
        out = pltpu.make_async_copy(normed_ref.at[part], normed_hbm.at[part], sems.at[count + c])
        out.start()
        outs.append(out)
        g = gelu_twice(dot(normed, first_ref[...]))
        total += jnp.sum(g.reshape(n * z_local, y_local, width), axis=0)
    sum_y_ref[...] = total
    for out in outs:
        out.wait()


def chunks_of(ref):
    n = ref.shape[0] // CHUNKS
    for c in range(CHUNKS):
        yield c * n, ref[pl.ds(c * n, n)].reshape(-1, ref.shape[3]), n


def sum_x_kernel(normed_ref, first_ref, sum_x_ref):
    for start, rows, n in chunks_of(normed_ref):
        g = gelu_twice(dot(rows, first_ref[...]))
        sum_x_ref[start : start + n, :] = jnp.sum(g.reshape(n, -1, g.shape[1]), axis=1)


def value_kernel(normed_ref, weight_ref, value_ref):
    z_local, y_local, width = normed_ref.shape[1:]
    for start, rows, n in chunks_of(normed_ref):
        value = dot(rows, weight_ref[...]).astype(BF16).reshape(n, z_local, y_local, width)
        for z in range(z_local):
            value_ref[start : start + n, :, z * width : (z + 1) * width] = value[:, z]


def outer_kernel(scale_x, scale_y, sum_x_ref, sum_y_ref, key_x_ref, key_y_ref, value_ref, total_ref, part_ref, rows_ref):
    x_local, y_local, lanes = value_ref.shape
    width = key_x_ref.shape[0]
    depth = width // H
    key_y = summary(sum_y_ref[...], scale_y, key_y_ref[...])
    left = jnp.concatenate(halves(key_y.T), axis=1)
    spread_into(rows_ref, summary(sum_x_ref[...], scale_x, key_x_ref[...]))
    head = (lax.broadcasted_iota(jnp.int32, (depth, lanes), 1) % width) // depth

    def step(j, carry):
        group = [j * GROUP + q for q in range(GROUP)]
        fulls = [dot(left, jnp.concatenate([value_ref[i]] * 2, axis=0)) for i in group]
        for i, full in zip(group, fulls):
            acc = full[:depth]
            for h in range(1, H):
                acc = jnp.where(head == h, full[h * depth : (h + 1) * depth], acc)
            part_ref[i] = acc
        return carry

    lax.fori_loop(0, x_local // GROUP, step, 0)

    for z in range(lanes // width):
        cols = slice(z * width, (z + 1) * width)
        for d in range(depth):
            acc = jnp.zeros((depth, width), F32)
            for i in range(x_local):
                acc += rows_ref[i : i + 1, d * width : (d + 1) * width] * part_ref[i, :, cols]
            total_ref[d * depth : (d + 1) * depth, cols] = acc.astype(BF16)


def query_kernel(scale_x, scale_y, sum_x_ref, sum_y_ref, query_x_ref, query_y_ref, left_ref, rows_ref):
    high, low = halves(summary(sum_y_ref[...], scale_y, query_y_ref[...]))
    left_ref[...] = jnp.concatenate(
        [jnp.concatenate([high, high], axis=1), jnp.concatenate([low, jnp.zeros_like(low)], axis=1)], axis=0
    )
    spread_into(rows_ref, summary(sum_x_ref[...], scale_x, query_x_ref[...]))


def finish_kernel(left_ref, rows_ref, total_ref, weight_ref, out_hbm, out_ref, wide_ref, sems):
    x_local, z_local, y_local, width = out_ref.shape
    depth = width // H
    lanes = z_local * width
    wide_ref[...] = total_ref[...].astype(F32)
    left = left_ref[...]
    head = (lax.broadcasted_iota(jnp.int32, (depth, lanes), 1) % width) // depth
    zero = jnp.zeros((depth, lanes), BF16)

    def copy_of(i):
        return pltpu.make_async_copy(out_ref.at[i], out_hbm.at[i], sems.at[i])

    def right_of(i):
        pieces = []
        rows = rows_ref[pl.ds(i, 1), :]
        for z in range(z_local):
            cols = slice(z * width, (z + 1) * width)
            acc = jnp.zeros((depth, width), F32)
            for d in range(depth):
                acc += rows[:, d * width : (d + 1) * width] * wide_ref[d * depth : (d + 1) * depth, cols]
            pieces.append(acc)
        return jnp.concatenate(
            [jnp.where(head == h, w, zero) for w in halves(jnp.concatenate(pieces, axis=1)) for h in range(H)],
            axis=0,
        )

    def step(j, carry):
        group = [j * WIDE_GROUP + q for q in range(WIDE_GROUP)]
        boths = [dot(left, right) for right in [right_of(i) for i in group]]
        for i, both in zip(group, boths):
            u = (both[:y_local] + both[y_local:]).astype(BF16)
            u = jnp.concatenate([u[:, z * width : (z + 1) * width] for z in range(z_local)], axis=0)
            out_ref[i] = dot(u, weight_ref[...]).astype(BF16).reshape(z_local, y_local, width)
            copy_of(i).start()
        return carry

    lax.fori_loop(0, x_local // WIDE_GROUP, step, 0)

    def finish(i, carry):
        copy_of(i).wait()
        return carry

    lax.fori_loop(0, x_local, finish, 0)


def call(kernel, out_shape, flops, scratch=(), limit=VMEM_LIMIT, **specs):
    return pl.pallas_call(
        kernel,
        out_shape=out_shape,
        scratch_shapes=list(scratch),
        compiler_params=pltpu.CompilerParams(vmem_limit_bytes=limit),
        cost_estimate=pl.CostEstimate(flops=flops, bytes_accessed=4 << 20, transcendentals=0),
        **specs,
    )


def sum_over(value, axis, stride, radix):
    total = value
    for k in range(1, radix):
        pairs = []
        for i in range(lax.axis_size(axis)):
            digit = i // stride % radix
            pairs.append((i, i + ((digit + k) % radix - digit) * stride))
        total = total + lax.ppermute(value, axis, pairs)
    return total


def digits(size):
    steps = []
    while size > 1:
        radix = 2 if size == 2 else 4
        size //= radix
        steps.append((size, radix))
    return steps


def sums_over(value, axis):
    for step in digits(lax.axis_size(axis)):
        value = sum_over(value, axis, *step)
    return value


def total_sum(part, beside, *args):
    axes = ("row", "col")
    rows_n, cols_n = lax.axis_size("row"), lax.axis_size("col")
    half = rows_n // 2
    n = half * cols_n
    groups = [[(k * half + r) * cols_n + c for r in range(half) for c in range(cols_n)] for k in range(2)]
    rows, lanes = part.shape
    blocks = lax.all_to_all(part.reshape(n, rows // n, lanes), axes, 0, 0, axis_index_groups=groups)
    mine = jnp.sum(blocks.astype(F32), axis=0)
    swap = [(r, (r + half) % rows_n) for r in range(rows_n)]
    mine, args = lax.optimization_barrier((mine, args))
    other = lax.ppermute(mine.astype(BF16), "row", swap)
    done = beside(*args)
    mine, done = lax.optimization_barrier(((mine + other.astype(F32)).astype(BF16), done))
    spread = jnp.broadcast_to(mine, blocks.shape)
    return lax.all_to_all(spread, axes, 0, 0, axis_index_groups=groups).reshape(rows, lanes), done


def body(field, norm_gain, first_x, second_x, first_y, second_y, value_weight, out_weight):
    x_local, y_local, z_local, width = field.shape
    depth = width // H
    lanes = z_local * width
    total_x = x_local * lax.axis_size("row")
    total_y = y_local * lax.axis_size("col")
    slab_shape = (x_local, z_local, y_local, width)
    sum_y, normed = call(
        norm_kernel,
        [jax.ShapeDtypeStruct((y_local, width), F32), jax.ShapeDtypeStruct(slab_shape, BF16)],
        1 << 30,
        [
            pltpu.VMEM(slab_shape, BF16),
            pltpu.VMEM(slab_shape, BF16),
            pltpu.VMEM((1, width), F32),
            pltpu.VMEM((width, width), BF16),
            pltpu.SemaphoreType.DMA((2 * len(CUTS),)),
        ],
        out_specs=[pl.BlockSpec(memory_space=pltpu.VMEM), IN_HBM],
        limit=LIMIT_A,
        in_specs=[IN_HBM] * 3,
    )(jnp.transpose(field, (0, 2, 1, 3)), norm_gain.reshape(1, width), first_y)
    sum_x = call(sum_x_kernel, jax.ShapeDtypeStruct((x_local, width), F32), 1 << 30)(normed, first_x)
    value = call(value_kernel, jax.ShapeDtypeStruct((x_local, y_local, lanes), BF16), 1 << 30)(normed, value_weight)
    sum_x = sums_over(sum_x, "col")
    sum_y = sums_over(sum_y, "row")
    mean_x = 0.5 / (total_y * z_local)
    mean_y = 0.5 / (total_x * z_local)
    part = call(
        functools.partial(outer_kernel, mean_x, mean_y),
        jax.ShapeDtypeStruct((depth * depth, lanes), BF16),
        1 << 30,
        [pltpu.VMEM((x_local, depth, lanes), F32), pltpu.VMEM((x_local, depth * width), F32)],
    )(sum_x, sum_y, second_x[:, width:], second_y[:, width:], value)
    queries = call(
        functools.partial(query_kernel, mean_x * total_x**-0.5, mean_y * total_y**-0.5),
        [
            jax.ShapeDtypeStruct((2 * y_local, 2 * width), BF16),
            jax.ShapeDtypeStruct((x_local, depth * width), F32),
        ],
        1 << 30,
    )
    total, (left, rows) = total_sum(part, queries, sum_x, sum_y, second_x[:, :width], second_y[:, :width])
    out = call(
        finish_kernel,
        jax.ShapeDtypeStruct(slab_shape, BF16),
        1 << 30,
        [
            pltpu.VMEM(slab_shape, BF16),
            pltpu.VMEM((depth * depth, lanes), F32),
            pltpu.SemaphoreType.DMA((x_local,)),
        ],
        out_specs=IN_HBM,
    )(left, rows, total, out_weight)
    return jnp.transpose(out, (0, 2, 1, 3))


def solution(mesh):
    placed = (P("row", "col", "zs", None), P(), P(), P(), P(), P(), P(), P())
    return jax.shard_map(
        body, mesh=mesh, in_specs=placed, out_specs=P("row", "col", "zs", None), check_vma=False
    )
```

```python
import functools

import jax
import jax.numpy as jnp
from jax import lax
from jax.experimental import pallas as pl
from jax.experimental.pallas import tpu as pltpu
from jax.sharding import PartitionSpec as P

H = 8
EPS = 1e-05
F32 = jnp.float32
BF16 = jnp.bfloat16
GELU_A = 0.7978845608028654
GELU_B = GELU_A * 0.044715
VMEM_LIMIT = 48 * 1024 * 1024
CHUNKS = 2
CUTS = (0, 2, 8, 14, 16)
GROUP = 8
WIDE_GROUP = 16
LIMIT_A = 62 * 1024 * 1024
IN_HBM = pl.BlockSpec(memory_space=pltpu.HBM)


def dot(a, b):
    return jnp.dot(a, b, preferred_element_type=F32)


def halves(a):
    high = a.astype(BF16)
    return high, (a - high.astype(F32)).astype(BF16)


def summary(sums, scale, second):
    return dot(jnp.concatenate(halves(sums * scale), axis=1), jnp.concatenate([second, second], axis=0))


def spread_into(ref, rows):
    width = rows.shape[1]
    depth = width // H
    start = lax.broadcasted_iota(jnp.int32, rows.shape, 1) // depth * depth
    for d in range(depth):
        ref[:, d * width : (d + 1) * width] = jnp.take_along_axis(rows, start + d, axis=1)


def gelu_twice(h):
    return h + h * jnp.tanh(h * (GELU_A + GELU_B * (h * h)))


def norm_kernel(field_hbm, gain_hbm, first_hbm, sum_y_ref, normed_hbm, field_ref, normed_ref, gain_ref, first_ref, sems):
    x_local, z_local, y_local, width = normed_ref.shape
    cuts = [x_local * k // 16 for k in CUTS]
    parts = [(a, b - a) for a, b in zip(cuts[:-1], cuts[1:])]
    count = len(parts)
    small = [
        pltpu.make_async_copy(gain_hbm, gain_ref, sems.at[2 * count]),
        pltpu.make_async_copy(first_hbm, first_ref, sems.at[2 * count + 1]),
    ]
    big = [
        pltpu.make_async_copy(field_hbm.at[pl.ds(a, n)], field_ref.at[pl.ds(a, n)], sems.at[c])
        for c, (a, n) in enumerate(parts)
    ]
    for copy in big[:1] + small + big[1:]:
        copy.start()
    total = jnp.zeros(sum_y_ref.shape, F32)
    ones = jnp.full((width, width), 1.0 / width, BF16)
    outs = []

    for c, (a, n) in enumerate(parts):
        big[c].wait()
        part = pl.ds(a, n)
        values = field_ref[part].reshape(n * z_local * y_local, width)
        centred = values.astype(F32) - dot(values, ones)
        spread = jnp.mean(centred * centred, axis=-1, keepdims=True)
        if c == 0:
            for copy in small:
                copy.wait()
        normed = (centred * lax.rsqrt(spread + EPS) * gain_ref[...]).astype(BF16)
        normed_ref[part] = normed.reshape(n, z_local, y_local, width)
        out = pltpu.make_async_copy(normed_ref.at[part], normed_hbm.at[part], sems.at[count + c])
        out.start()
        outs.append(out)
        g = gelu_twice(dot(normed, first_ref[...]))
        total += jnp.sum(g.reshape(n * z_local, y_local, width), axis=0)
    sum_y_ref[...] = total
    for out in outs:
        out.wait()


def chunks_of(ref):
    n = ref.shape[0] // CHUNKS
    for c in range(CHUNKS):
        yield c * n, ref[pl.ds(c * n, n)].reshape(-1, ref.shape[3]), n


def sum_x_kernel(normed_ref, first_ref, sum_x_ref):
    for start, rows, n in chunks_of(normed_ref):
        g = gelu_twice(dot(rows, first_ref[...]))
        sum_x_ref[start : start + n, :] = jnp.sum(g.reshape(n, -1, g.shape[1]), axis=1)


def value_kernel(normed_ref, weight_ref, value_ref):
    z_local, y_local, width = normed_ref.shape[1:]
    for start, rows, n in chunks_of(normed_ref):
        value = dot(rows, weight_ref[...]).astype(BF16).reshape(n, z_local, y_local, width)
        for z in range(z_local):
            value_ref[start : start + n, :, z * width : (z + 1) * width] = value[:, z]


def outer_kernel(scale_x, scale_y, sum_x_ref, sum_y_ref, key_x_ref, key_y_ref, value_ref, total_ref, part_ref, rows_ref):
    x_local, y_local, lanes = value_ref.shape
    width = key_x_ref.shape[0]
    depth = width // H
    key_y = summary(sum_y_ref[...], scale_y, key_y_ref[...])
    left = jnp.concatenate(halves(key_y.T), axis=1)
    spread_into(rows_ref, summary(sum_x_ref[...], scale_x, key_x_ref[...]))
    head = (lax.broadcasted_iota(jnp.int32, (depth, lanes), 1) % width) // depth

    def step(j, carry):
        group = [j * GROUP + q for q in range(GROUP)]
        fulls = [dot(left, jnp.concatenate([value_ref[i]] * 2, axis=0)) for i in group]
        for i, full in zip(group, fulls):
            acc = full[:depth]
            for h in range(1, H):
                acc = jnp.where(head == h, full[h * depth : (h + 1) * depth], acc)
            part_ref[i] = acc
        return carry

    lax.fori_loop(0, x_local // GROUP, step, 0)

    for z in range(lanes // width):
        cols = slice(z * width, (z + 1) * width)
        for d in range(depth):
            acc = jnp.zeros((depth, width), F32)
            for i in range(x_local):
                acc += rows_ref[i : i + 1, d * width : (d + 1) * width] * part_ref[i, :, cols]
            total_ref[d * depth : (d + 1) * depth, cols] = acc.astype(BF16)


def query_kernel(scale_x, scale_y, sum_x_ref, sum_y_ref, query_x_ref, query_y_ref, left_ref, rows_ref):
    high, low = halves(summary(sum_y_ref[...], scale_y, query_y_ref[...]))
    left_ref[...] = jnp.concatenate(
        [jnp.concatenate([high, high], axis=1), jnp.concatenate([low, jnp.zeros_like(low)], axis=1)], axis=0
    )
    spread_into(rows_ref, summary(sum_x_ref[...], scale_x, query_x_ref[...]))


def finish_kernel(left_ref, rows_ref, total_ref, weight_ref, out_hbm, out_ref, wide_ref, sems):
    x_local, z_local, y_local, width = out_ref.shape
    depth = width // H
    lanes = z_local * width
    wide_ref[...] = total_ref[...].astype(F32)
    left = left_ref[...]
    head = (lax.broadcasted_iota(jnp.int32, (depth, lanes), 1) % width) // depth
    zero = jnp.zeros((depth, lanes), BF16)

    def copy_of(i):
        return pltpu.make_async_copy(out_ref.at[i], out_hbm.at[i], sems.at[i])

    def right_of(i):
        pieces = []
        rows = rows_ref[pl.ds(i, 1), :]
        for z in range(z_local):
            cols = slice(z * width, (z + 1) * width)
            acc = jnp.zeros((depth, width), F32)
            for d in range(depth):
                acc += rows[:, d * width : (d + 1) * width] * wide_ref[d * depth : (d + 1) * depth, cols]
            pieces.append(acc)
        return jnp.concatenate(
            [jnp.where(head == h, w, zero) for w in halves(jnp.concatenate(pieces, axis=1)) for h in range(H)],
            axis=0,
        )

    def step(j, carry):
        group = [j * WIDE_GROUP + q for q in range(WIDE_GROUP)]
        boths = [dot(left, right) for right in [right_of(i) for i in group]]
        for i, both in zip(group, boths):
            u = (both[:y_local] + both[y_local:]).astype(BF16)
            u = jnp.concatenate([u[:, z * width : (z + 1) * width] for z in range(z_local)], axis=0)
            out_ref[i] = dot(u, weight_ref[...]).astype(BF16).reshape(z_local, y_local, width)
            copy_of(i).start()
        return carry

    lax.fori_loop(0, x_local // WIDE_GROUP, step, 0)

    def finish(i, carry):
        copy_of(i).wait()
        return carry

    lax.fori_loop(0, x_local, finish, 0)


def call(kernel, out_shape, flops, scratch=(), limit=VMEM_LIMIT, **specs):
    return pl.pallas_call(
        kernel,
        out_shape=out_shape,
        scratch_shapes=list(scratch),
        compiler_params=pltpu.CompilerParams(vmem_limit_bytes=limit),
        cost_estimate=pl.CostEstimate(flops=flops, bytes_accessed=4 << 20, transcendentals=0),
        **specs,
    )


def sum_over(value, axis, stride, radix):
    total = value
    for k in range(1, radix):
        pairs = []
        for i in range(lax.axis_size(axis)):
            digit = i // stride % radix
            pairs.append((i, i + ((digit + k) % radix - digit) * stride))
        total = total + lax.ppermute(value, axis, pairs)
    return total


def digits(size):
    steps = []
    while size > 1:
        radix = 2 if size == 2 else 4
        size //= radix
        steps.append((size, radix))
    return steps


def sums_over(value, axis):
    for step in digits(lax.axis_size(axis)):
        value = sum_over(value, axis, *step)
    return value


def total_sum(part, beside, *args):
    axes = ("row", "col")
    rows_n, cols_n = lax.axis_size("row"), lax.axis_size("col")
    half = rows_n // 2
    n = half * cols_n
    groups = [[(k * half + r) * cols_n + c for r in range(half) for c in range(cols_n)] for k in range(2)]
    rows, lanes = part.shape
    blocks = lax.all_to_all(part.reshape(n, rows // n, lanes), axes, 0, 0, axis_index_groups=groups)
    mine = jnp.sum(blocks.astype(F32), axis=0)
    swap = [(r, (r + half) % rows_n) for r in range(rows_n)]
    mine, args = lax.optimization_barrier((mine, args))
    other = lax.ppermute(mine.astype(BF16), "row", swap)
    done = beside(*args)
    mine, done = lax.optimization_barrier(((mine + other.astype(F32)).astype(BF16), done))
    spread = jnp.broadcast_to(mine, blocks.shape)
    return lax.all_to_all(spread, axes, 0, 0, axis_index_groups=groups).reshape(rows, lanes), done


def body(field, norm_gain, first_x, second_x, first_y, second_y, value_weight, out_weight):
    x_local, y_local, z_local, width = field.shape
    depth = width // H
    lanes = z_local * width
    total_x = x_local * lax.axis_size("row")
    total_y = y_local * lax.axis_size("col")
    slab_shape = (x_local, z_local, y_local, width)
    sum_y, normed = call(
        norm_kernel,
        [jax.ShapeDtypeStruct((y_local, width), F32), jax.ShapeDtypeStruct(slab_shape, BF16)],
        1 << 30,
        [
            pltpu.VMEM(slab_shape, BF16),
            pltpu.VMEM(slab_shape, BF16),
            pltpu.VMEM((1, width), F32),
            pltpu.VMEM((width, width), BF16),
            pltpu.SemaphoreType.DMA((2 * len(CUTS),)),
        ],
        out_specs=[pl.BlockSpec(memory_space=pltpu.VMEM), IN_HBM],
        limit=LIMIT_A,
        in_specs=[IN_HBM] * 3,
    )(jnp.transpose(field, (0, 2, 1, 3)), norm_gain.reshape(1, width), first_y)
    sum_x = call(sum_x_kernel, jax.ShapeDtypeStruct((x_local, width), F32), 1 << 30)(normed, first_x)
    value = call(value_kernel, jax.ShapeDtypeStruct((x_local, y_local, lanes), BF16), 1 << 30)(normed, value_weight)
    sum_x = sums_over(sum_x, "col")
    sum_y = sums_over(sum_y, "row")
    mean_x = 0.5 / (total_y * z_local)
    mean_y = 0.5 / (total_x * z_local)
    part = call(
        functools.partial(outer_kernel, mean_x, mean_y),
        jax.ShapeDtypeStruct((depth * depth, lanes), BF16),
        1 << 30,
        [pltpu.VMEM((x_local, depth, lanes), F32), pltpu.VMEM((x_local, depth * width), F32)],
    )(sum_x, sum_y, second_x[:, width:], second_y[:, width:], value)
    queries = call(
        functools.partial(query_kernel, mean_x * total_x**-0.5, mean_y * total_y**-0.5),
        [
            jax.ShapeDtypeStruct((2 * y_local, 2 * width), BF16),
            jax.ShapeDtypeStruct((x_local, depth * width), F32),
        ],
        1 << 30,
    )
    total, (left, rows) = total_sum(part, queries, sum_x, sum_y, second_x[:, :width], second_y[:, :width])
    out = call(
        finish_kernel,
        jax.ShapeDtypeStruct(slab_shape, BF16),
        1 << 30,
        [
            pltpu.VMEM(slab_shape, BF16),
            pltpu.VMEM((depth * depth, lanes), F32),
            pltpu.SemaphoreType.DMA((x_local,)),
        ],
        out_specs=IN_HBM,
    )(left, rows, total, out_weight)
    return jnp.transpose(out, (0, 2, 1, 3))


def solution(mesh):
    placed = (P("row", "col", "zs", None), P(), P(), P(), P(), P(), P(), P())
    return jax.shard_map(
        body, mesh=mesh, in_specs=placed, out_specs=P("row", "col", "zs", None), check_vma=False
    )
```
